512 devices in a mesh: chol: 128 (over y, z_lo, x, core), orb: 4 (over z_hi).
Axes of the slice: x: 4, y: 4, z: 16 (z_hi: 4, z_lo: 4; z = z_hi * 4 + z_lo), core: 2. Of those that a mesh axis runs over, the one named last changes fastest.
Arguments:
- half_green: bfloat16 [128, 64, 512], P('chol', None, 'orb'), may hold values from -6 to 6
- rotated_chol: bfloat16 [2560, 64, 512], P('chol', None, 'orb'), may hold values from -0.03125 to 0.03125
- chol_vectors: bfloat16 [2560, 512, 512], P('chol', 'orb'), may hold values from -0.0048828125 to 0.0048828125
- walkers: bfloat16 [128, 64, 512], P('chol', None, 'orb'), may hold values from -6 to 6
- field_levels: int32 [128, 2560], P(None, 'chol'), may hold values from -1 to 1
Outputs:
- force_bias: float32 [128, 2560], P(None, 'chol')
- new_walkers: bfloat16 [128, 64, 512], P('chol', None, 'orb')
The draws below stay inside these ranges and needn't reach their ends.
Inputs may be any that keep to these rules, and one draw needn't show every extreme that they name: `field_levels`: each entry is -1, 0 or 1.
All inputs are finite; a program needn't handle non-finite values.
Results may differ from the reference program's by a relative error of at most 0.007.
Values may be sent and summed in bfloat16 or wider, within the bound.
No kernel may reach another device: no remote copies, remote signals or barrier semaphores. Data moves between devices by JAX's collectives and lax.ppermute only.
A program may use at most 64 MiB of HBM per device.

```python
import jax
import jax.numpy as jnp
from jax import lax

M = 512
N = 64
NCHOL = 2560
WALKERS = 128


def plant(array, stream_key, low, high):
    index_at = [jax.random.randint(jax.random.fold_in(stream_key, axis), (), 0, length) for axis, length in enumerate(array.shape)]
    longest = array.shape.index(max(array.shape))
    neighbour = index_at[:longest] + [(index_at[longest] + 1) % array.shape[longest]] + index_at[longest + 1:]
    return array.at[tuple(index_at)].set(low).at[tuple(neighbour)].set(high)


def steps_of(stream_key, extent, split, smallest, top_value):
    gain = 1.0
    for position, shards_of in split:
        heights = jax.random.uniform(jax.random.fold_in(jax.random.fold_in(stream_key, 6), position), (shards_of,), jnp.float32, smallest / len(split), top_value / len(split))
        gain = gain * jnp.repeat(jnp.exp(heights), extent[position] // shards_of).reshape((-1,) + (1,) * (len(extent) - 1 - position))
    return gain


def scatter_about(stream_key, shape, spread, most, split=(), held_as=jnp.bfloat16):
    result = spread * jax.random.normal(stream_key, shape, jnp.float32)
    if split:
        result = result * steps_of(stream_key, shape, split, -0.22, 0.18)
    return jnp.clip(result, -most, most).astype(held_as)


def setup_inputs(seed: int = 0) -> dict:
    key_of = jax.random.split(jax.random.key(seed), 6)
    half_green = scatter_about(key_of[0], (WALKERS, N, M), 1.0, 6.0, ((0, 128), (2, 4)))
    rotated_chol = scatter_about(key_of[1], (NCHOL, N, M), (N * M) ** -0.5, 0.03125, ((0, 128), (2, 4)))
    chol_vectors = scatter_about(key_of[2], (NCHOL, M, M), (NCHOL * M) ** -0.5, 0.0048828125, ((0, 128), (1, 4)))
    walkers = scatter_about(key_of[3], (WALKERS, N, M), 1.0, 6.0, ((0, 128), (2, 4)))
    field_levels = plant(jax.random.randint(key_of[4], (WALKERS, NCHOL), -1, 2), jax.random.fold_in(key_of[4], 1), -1, 1).astype(jnp.int32)
    return {"half_green": half_green, "rotated_chol": rotated_chol, "chol_vectors": chol_vectors, "walkers": walkers, "field_levels": field_levels}


LEVEL_SCALE = 1.7320508
TAU_ROOT = 0.2236068


def reference(half_green, rotated_chol, chol_vectors, walkers, field_levels):
    force_bias = jnp.einsum('giq,wiq->wg', rotated_chol.astype(jnp.float32), half_green.astype(jnp.float32), precision=lax.Precision.HIGHEST)
    aux_field = (LEVEL_SCALE * field_levels.astype(jnp.float32) - TAU_ROOT * force_bias).astype(jnp.bfloat16)
    chol_flat = chol_vectors.reshape(NCHOL, M * M)
    block_rows = 8 if WALKERS % 8 == 0 else 1
    num_blocks = WALKERS // block_rows

    def one_block(operands):
        block_fields, block_walkers = operands
        potential = jnp.dot(block_fields, chol_flat, preferred_element_type=jnp.float32).reshape(block_rows, M, M)
        potential = lax.optimization_barrier(potential.astype(jnp.bfloat16)).astype(jnp.float32)
        return jnp.einsum('wiq,wpq->wip', block_walkers.astype(jnp.float32), potential, precision=lax.Precision.HIGHEST)

    applied = lax.map(one_block, (aux_field.reshape(num_blocks, block_rows, NCHOL), walkers.reshape(num_blocks, block_rows, N, M)))
    applied = applied.reshape(WALKERS, N, M)
    new_walkers = (walkers.astype(jnp.float32) - TAU_ROOT * applied).astype(jnp.bfloat16)
    return force_bias, new_walkers
```

```python
import jax
import jax.numpy as jnp
from jax import lax
from jax.sharding import PartitionSpec as P

LEVEL_SCALE = 1.7320508
TAU_ROOT = 0.2236068

SIDE = 4
CORES = 2
CHIPS = SIDE**3
PLANE = SIDE * SIDE
PAD_ROWS = 24


def chol_index(y, z, x, core):
    return ((y * SIDE + z) * SIDE + x) * CORES + core


SAME_CORE = [[CORES * chip + core for chip in range(CHIPS)] for core in range(CORES)]
SAME_PLANE = [
    [chol_index(y, z, x, core) for y in range(SIDE) for x in range(SIDE)]
    for z in range(SIDE)
    for core in range(CORES)
]
OTHER_CORE = [(i, i ^ 1) for i in range(CHIPS * CORES)]


def to_all(block, groups):
    copies = jnp.broadcast_to(block[None], (len(groups[0]),) + block.shape)
    return lax.all_to_all(copies, "chol", 0, 0, axis_index_groups=groups)


def shards(half_green, rotated_chol, chol_vectors, walkers, field_levels):
    f32, bf16 = jnp.float32, jnp.bfloat16
    own, own_rows, basis = chol_vectors.shape
    number = field_levels.shape[0]
    core = lax.axis_index("chol") % CORES
    rows = own_rows // PLANE
    swap = lambda array: lax.ppermute(array, "chol", OTHER_CORE)

    green = to_all(half_green[0], SAME_CORE)
    rotated_other = swap(rotated_chol)

    chol_rows = chol_vectors.reshape(own, PLANE, rows * basis).transpose(1, 0, 2)
    chol_rows = jnp.pad(chol_rows, ((0, 0), (0, PAD_ROWS - own), (0, 0)))
    chol_own = lax.all_to_all(chol_rows, "chol", 0, 0, axis_index_groups=SAME_PLANE)
    chol_own = chol_own.reshape(PLANE * PAD_ROWS, rows * basis)
    chol_other = swap(chol_own)

    levels = field_levels.astype(bf16).reshape(number // CORES, CORES, own)
    levels_own = lax.dynamic_index_in_dim(levels, core, 1, keepdims=False)
    levels_sent = lax.dynamic_index_in_dim(levels, 1 - core, 1, keepdims=False)
    levels_got = swap(levels_sent)
    levels_both = jnp.concatenate([levels_own.T, levels_got.T], axis=1)

    bias_parts = [
        jnp.einsum("giq,wiq->gw", part, green, preferred_element_type=f32)
        for part in (rotated_chol, rotated_other)
    ]
    partial_bias = jnp.concatenate(bias_parts, axis=1).astype(bf16)
    gathered = lax.all_gather(
        jnp.concatenate([partial_bias, walkers[0]], axis=0), "orb", axis=0, tiled=False
    )
    bias = jnp.sum(gathered[:, :own].astype(f32), axis=0)
    walker_full = gathered[:, own:]

    aux_field = (LEVEL_SCALE * levels_both.astype(f32) - TAU_ROOT * bias).astype(bf16)
    aux_field = jnp.pad(aux_field, ((0, PAD_ROWS - own), (0, 0)))
    aux_all = to_all(aux_field, SAME_PLANE).reshape(PLANE * PAD_ROWS, number)
    half = number // CORES
    contract_rows = (((0,), (0,)), ((), ()))
    potential = lax.dot_general(
        aux_all[:, :half], chol_own, contract_rows, preferred_element_type=f32
    ) + lax.dot_general(
        aux_all[:, half:], chol_other, contract_rows, preferred_element_type=f32
    )
    potential = potential.astype(bf16).reshape(CHIPS, rows, basis)
    parts = lax.all_to_all(potential, "chol", 0, 0, axis_index_groups=SAME_CORE)
    parts = parts.reshape(SIDE, SIDE, SIDE, rows, basis)
    total = jnp.sum(parts.astype(f32), axis=1).astype(bf16).reshape(own_rows, basis)
    applied = jnp.einsum(
        "biq,pbq->ip",
        walker_full,
        total.reshape(own_rows, walker_full.shape[0], walker_full.shape[2]),
        preferred_element_type=f32,
    )
    new_walkers = (walkers[0].astype(f32) - TAU_ROOT * applied).astype(bf16)[None]

    bias_got = swap(bias[:, half:])
    bias_own = bias[:, :half]
    pair = jnp.stack(
        [jnp.where(core == 0, bias_own, bias_got), jnp.where(core == 0, bias_got, bias_own)],
        axis=2,
    )
    force_bias = pair.reshape(own, number).T
    return (force_bias, new_walkers)


def solution(mesh):
    placed = (
        P("chol", None, "orb"),
        P("chol", None, "orb"),
        P("chol", "orb", None),
        P("chol", None, "orb"),
        P(None, "chol"),
    )
    return jax.shard_map(
        shards,
        mesh=mesh,
        in_specs=placed,
        out_specs=(P(None, "chol"), P("chol", None, "orb")),
        check_vma=False,
    )
```

```python
import jax
import jax.numpy as jnp
import numpy as np
from jax import lax
from jax.sharding import PartitionSpec as P

LEVEL_SCALE = 1.7320508
TAU_ROOT = 0.2236068

SIDE = 4
MATES = 4
PLACES = [
    (y, zh, zl, x, core)
    for y in range(SIDE)
    for zh in range(2)
    for zl in range(2)
    for x in range(SIDE)
    for core in range(2)
]


def groups_of(fixed, order):
    found = {}
    for index, place in enumerate(PLACES):
        key = tuple(place[i] for i in fixed)
        found.setdefault(key, []).append((tuple(place[i] for i in order), index))
    return [[index for _, index in sorted(members)] for members in found.values()]


Y, ZH, ZL, X, CORE = range(5)
GREEN = groups_of((ZL, CORE), (Y, ZH, X))
PLANE = groups_of((ZH, ZL, CORE), (Y, X))
BLOCK = groups_of((ZH, CORE), (Y, X, ZL))
HOME = groups_of((CORE,), (ZL, Y, ZH, X))
HOMES = len(HOME[0])
CHIPS = len(PLANE[0])
SHARES = np.zeros((MATES, len(PLACES), len(GREEN[0])), np.float32)
for group in GREEN:
    first = PLACES[group[0]]
    SHARES[first[ZL] * 2 + first[CORE], group, np.arange(len(group))] = 1


def to_mate(array, number):
    step = (number & 1) + (number >> 1) * 2 * SIDE
    return lax.ppermute(array, "chol", [(i, i ^ step) for i in range(len(PLACES))])


def shards(half_green, rotated_chol, chol_vectors, walkers, field_levels):
    f32, bf16 = jnp.float32, jnp.bfloat16
    own, own_rows, basis = chol_vectors.shape
    number = field_levels.shape[0]
    occupied, width = walkers.shape[1], walkers.shape[2]
    share = number // MATES
    rows = own_rows // CHIPS
    index = lax.axis_index("chol")
    core = index % 2
    zl = index // (2 * SIDE) % 2

    def by_number(array):
        array = array.reshape((2, 2) + array.shape[1:])
        array = jnp.where(core == 0, array, jnp.stack([array[:, 1], array[:, 0]], axis=1))
        return jnp.where(zl == 0, array, jnp.stack([array[1], array[0]], axis=0))

    green = jnp.broadcast_to(half_green, (len(GREEN[0]), occupied, width))
    green = lax.all_to_all(green, "chol", 0, 0, axis_index_groups=GREEN)

    levels = jnp.pad(field_levels.astype(bf16).T, ((0, occupied - own), (0, 0)))
    sent = jnp.concatenate([rotated_chol, levels[None]], axis=0)
    held = [sent, to_mate(sent, 1), to_mate(sent, 2)]
    held.append(to_mate(held[2], 1))
    levels = jnp.concatenate([h[own, : own + 1] for h in held], axis=0)
    chosen = lax.dynamic_index_in_dim(jnp.asarray(SHARES, bf16), zl * 2 + core, 0, keepdims=False)
    levels = jnp.dot(levels, chosen, preferred_element_type=f32)

    chol_rows = chol_vectors.reshape(own, CHIPS, 2, rows // 2 * basis).transpose(1, 0, 2, 3)
    chol_rows = chol_rows.reshape(CHIPS, own * 2, rows // 2 * basis)

    green, chol_rows, levels, held = lax.optimization_barrier((green, chol_rows, levels, held))
    chol_mine = lax.all_to_all(chol_rows, "chol", 0, 0, axis_index_groups=PLANE)
    chol_mine = chol_mine.reshape(CHIPS * own * 2, rows // 2 * basis)

    rotated = jnp.concatenate(held, axis=0)
    partial_bias = jnp.einsum("giq,wiq->gw", rotated, green, preferred_element_type=f32)
    partial_bias = jnp.pad(partial_bias.astype(bf16), ((0, 0), (0, width - share)))
    gathered = lax.all_gather(
        jnp.concatenate([walkers[0], partial_bias], axis=0), "orb", axis=0, tiled=False
    )
    bias = jnp.sum(gathered[:, occupied:, :share].astype(f32), axis=0)
    walker_full = gathered[:, :occupied]
    bias, chol_mine, walker_full = lax.optimization_barrier((bias, chol_mine, walker_full))

    aux_field = (LEVEL_SCALE * levels - TAU_ROOT * bias).astype(bf16)
    aux_field = aux_field.reshape(2, 2, own + 1, share)[:, :, :own]
    aux_field = jnp.where(zl == 0, aux_field, jnp.stack([aux_field[1], aux_field[0]]))
    zero = jnp.zeros_like(aux_field)
    aux_field = jnp.stack(
        [jnp.concatenate([aux_field, zero], axis=3), jnp.concatenate([zero, aux_field], axis=3)],
        axis=3,
    ).reshape(2, 2 * own * 2, 2 * share)
    aux_sent = jnp.broadcast_to(aux_field[None], (CHIPS,) + aux_field.shape)
    aux_sent = aux_sent.reshape((CHIPS * 2,) + aux_field.shape[1:])
    aux_all = lax.all_to_all(aux_sent, "chol", 0, 0, axis_index_groups=BLOCK)
    aux_all = aux_all.reshape(CHIPS, 2, 2, own * 2, 2 * share)
    aux_all = jnp.concatenate([aux_all[:, 0], aux_all[:, 1]], axis=3)
    chol_others = to_mate(chol_mine, 1)
    potential = sum(
        lax.dot_general(
            aux_all[:, i].reshape(CHIPS * own * 2, 4 * share),
            part,
            (((0,), (0,)), ((), ())),
            preferred_element_type=f32,
        )
        for i, part in enumerate((chol_mine, chol_others))
    )
    potential = potential.astype(bf16).reshape(2, 2, share, rows // 2 * basis)
    potential = potential.transpose(0, 2, 1, 3).reshape(HOMES, rows, basis)
    parts = lax.all_to_all(potential, "chol", 0, 0, axis_index_groups=HOME)
    parts = parts.reshape(2, SIDE, 2, SIDE, rows, basis)
    total = jnp.sum(parts.astype(f32), axis=(0, 2)).astype(bf16)

    applied = jnp.einsum(
        "biq,pbq->ip",
        walker_full,
        total.reshape(own_rows, basis // width, width),
        preferred_element_type=f32,
    )
    new_walkers = (walkers[0].astype(f32) - TAU_ROOT * applied).astype(bf16)[None]

    bias = bias.reshape(MATES, own + 1, share)[:, :own]
    bias = [bias[0]] + [to_mate(bias[r], r) for r in range(1, MATES)]
    bias = by_number(jnp.stack(bias)).reshape(2, 2, own, SIDE, 2, SIDE)
    force_bias = bias.transpose(3, 4, 0, 5, 1, 2).reshape(number, own)
    return (force_bias, new_walkers)


def solution(mesh):
    placed = (
        P("chol", None, "orb"),
        P("chol", None, "orb"),
        P("chol", "orb", None),
        P("chol", None, "orb"),
        P(None, "chol"),
    )
    return jax.shard_map(
        shards,
        mesh=mesh,
        in_specs=placed,
        out_specs=(P(None, "chol"), P("chol", None, "orb")),
        check_vma=False,
    )
```

```python
import jax
import jax.numpy as jnp
import numpy as np
from jax import lax
from jax.sharding import PartitionSpec as P

LEVEL_SCALE = 1.7320508
TAU_ROOT = 0.2236068

SIDE = 4
MATES = 4
PLACES = [
    (y, zh, zl, x, core)
    for y in range(SIDE)
    for zh in range(2)
    for zl in range(2)
    for x in range(SIDE)
    for core in range(2)
]


def groups_of(fixed, order):
    found = {}
    for index, place in enumerate(PLACES):
        key = tuple(place[i] for i in fixed)
        found.setdefault(key, []).append((tuple(place[i] for i in order), index))
    return [[index for _, index in sorted(members)] for members in found.values()]


Y, ZH, ZL, X, CORE = range(5)
GREEN = groups_of((ZL, CORE), (Y, ZH, X))
PLANE = groups_of((ZH, ZL, CORE), (Y, X))
BLOCK = groups_of((ZH, CORE), (Y, X, ZL))
HOME = groups_of((CORE,), (ZL, Y, ZH, X))
HOMES = len(HOME[0])
CHIPS = len(PLANE[0])
SHARES = np.zeros((MATES, len(PLACES), len(GREEN[0])), np.float32)
for group in GREEN:
    first = PLACES[group[0]]
    SHARES[first[ZL] * 2 + first[CORE], group, np.arange(len(group))] = 1


def to_mate(array, number):
    step = (number & 1) + (number >> 1) * 2 * SIDE
    return lax.ppermute(array, "chol", [(i, i ^ step) for i in range(len(PLACES))])


def shards(half_green, rotated_chol, chol_vectors, walkers, field_levels):
    f32, bf16 = jnp.float32, jnp.bfloat16
    own, own_rows, basis = chol_vectors.shape
    number = field_levels.shape[0]
    occupied, width = walkers.shape[1], walkers.shape[2]
    share = number // MATES
    rows = own_rows // CHIPS
    index = lax.axis_index("chol")
    core = index % 2
    zl = index // (2 * SIDE) % 2

    def by_number(array):
        array = array.reshape((2, 2) + array.shape[1:])
        array = jnp.where(core == 0, array, jnp.stack([array[:, 1], array[:, 0]], axis=1))
        return jnp.where(zl == 0, array, jnp.stack([array[1], array[0]], axis=0))

    green = jnp.broadcast_to(half_green, (len(GREEN[0]), occupied, width))
    green = lax.all_to_all(green, "chol", 0, 0, axis_index_groups=GREEN)

    levels = jnp.pad(field_levels.astype(bf16).T, ((0, occupied - own), (0, 0)))
    sent = jnp.concatenate([rotated_chol, levels[None]], axis=0)
    held = [sent, to_mate(sent, 1), to_mate(sent, 2)]

    chol_rows = chol_vectors.reshape(own, CHIPS, 2, rows // 2 * basis).transpose(1, 0, 2, 3)
    chol_rows = chol_rows.reshape(CHIPS, own * 2, rows // 2 * basis)

    green, chol_rows, held = lax.optimization_barrier((green, chol_rows, held))
    chol_mine = lax.all_to_all(chol_rows, "chol", 0, 0, axis_index_groups=PLANE)
    chol_mine = chol_mine.reshape(CHIPS * own * 2, rows // 2 * basis)

    held.append(to_mate(held[2], 1))
    levels = jnp.concatenate([h[own, : own + 1] for h in held], axis=0)
    chosen = lax.dynamic_index_in_dim(jnp.asarray(SHARES, bf16), zl * 2 + core, 0, keepdims=False)
    levels = jnp.dot(levels, chosen, preferred_element_type=f32)

    rotated = jnp.concatenate(held, axis=0)
    partial_bias = jnp.einsum("giq,wiq->gw", rotated, green, preferred_element_type=f32)
    partial_bias = jnp.pad(partial_bias.astype(bf16), ((0, 0), (0, width - share)))
    gathered = lax.all_gather(
        jnp.concatenate([walkers[0], partial_bias], axis=0), "orb", axis=0, tiled=False
    )
    bias = jnp.sum(gathered[:, occupied:, :share].astype(f32), axis=0)
    walker_full = gathered[:, :occupied]
    bias, chol_mine, walker_full = lax.optimization_barrier((bias, chol_mine, walker_full))

    aux_field = (LEVEL_SCALE * levels - TAU_ROOT * bias).astype(bf16)
    aux_field = aux_field.reshape(2, 2, own + 1, share)[:, :, :own]
    aux_field = jnp.where(zl == 0, aux_field, jnp.stack([aux_field[1], aux_field[0]]))
    zero = jnp.zeros_like(aux_field)
    aux_field = jnp.stack(
        [jnp.concatenate([aux_field, zero], axis=3), jnp.concatenate([zero, aux_field], axis=3)],
        axis=3,
    ).reshape(2, 2 * own * 2, 2 * share)
    aux_sent = jnp.broadcast_to(aux_field[None], (CHIPS,) + aux_field.shape)
    aux_sent = aux_sent.reshape((CHIPS * 2,) + aux_field.shape[1:])
    aux_all = lax.all_to_all(aux_sent, "chol", 0, 0, axis_index_groups=BLOCK)
    aux_all = aux_all.reshape(CHIPS, 2, 2, own * 2, 2 * share)
    aux_all = jnp.concatenate([aux_all[:, 0], aux_all[:, 1]], axis=3)
    chol_others = to_mate(chol_mine, 1)
    potential = sum(
        lax.dot_general(
            aux_all[:, i].reshape(CHIPS * own * 2, 4 * share),
            part,
            (((0,), (0,)), ((), ())),
            preferred_element_type=f32,
        )
        for i, part in enumerate((chol_mine, chol_others))
    )
    potential = potential.astype(bf16).reshape(2, 2, share, rows // 2 * basis)
    potential = potential.transpose(0, 2, 1, 3).reshape(HOMES, rows, basis)
    parts = lax.all_to_all(potential, "chol", 0, 0, axis_index_groups=HOME)
    parts = parts.reshape(2, SIDE, 2, SIDE, rows, basis)
    total = jnp.sum(parts.astype(f32), axis=(0, 2)).astype(bf16)

    applied = jnp.einsum(
        "biq,pbq->ip",
        walker_full,
        total.reshape(own_rows, basis // width, width),
        preferred_element_type=f32,
    )
    new_walkers = (walkers[0].astype(f32) - TAU_ROOT * applied).astype(bf16)[None]

    bias = bias.reshape(MATES, own + 1, share)[:, :own]
    bias = [bias[0]] + [to_mate(bias[r], r) for r in range(1, MATES)]
    bias = by_number(jnp.stack(bias)).reshape(2, 2, own, SIDE, 2, SIDE)
    force_bias = bias.transpose(3, 4, 0, 5, 1, 2).reshape(number, own)
    return (force_bias, new_walkers)


def solution(mesh):
    placed = (
        P("chol", None, "orb"),
        P("chol", None, "orb"),
        P("chol", "orb", None),
        P("chol", None, "orb"),
        P(None, "chol"),
    )
    return jax.shard_map(
        shards,
        mesh=mesh,
        in_specs=placed,
        out_specs=(P(None, "chol"), P("chol", None, "orb")),
        check_vma=False,
    )
```

```python
import jax
import jax.numpy as jnp
import numpy as np
from jax import lax
from jax.experimental.layout import Layout, with_layout_constraint
from jax.sharding import PartitionSpec as P

LEVEL_SCALE = 1.7320508
TAU_ROOT = 0.2236068

SIDE = 4
MATES = 4
PLACES = [
    (y, zh, zl, x, core)
    for y in range(SIDE)
    for zh in range(2)
    for zl in range(2)
    for x in range(SIDE)
    for core in range(2)
]


def groups_of(fixed, order):
    found = {}
    for index, place in enumerate(PLACES):
        key = tuple(place[i] for i in fixed)
        found.setdefault(key, []).append((tuple(place[i] for i in order), index))
    return [[index for _, index in sorted(members)] for members in found.values()]


Y, ZH, ZL, X, CORE = range(5)
GREEN = groups_of((ZL, CORE), (Y, ZH, X))
PLANE = groups_of((ZH, ZL, CORE), (Y, X))
BLOCK = groups_of((ZH, CORE), (Y, ZL, X))
HOME = groups_of((CORE,), (Y, ZH, ZL, X))
HOMES = len(HOME[0])
CHIPS = len(PLANE[0])
SHARES = np.zeros((MATES, len(PLACES), len(GREEN[0])), np.float32)
for group in GREEN:
    first = PLACES[group[0]]
    SHARES[first[ZL] * 2 + first[CORE], group, np.arange(len(group))] = 1


def to_mate(array, number):
    step = (number & 1) + (number >> 1) * 2 * SIDE
    return lax.ppermute(array, "chol", [(i, i ^ step) for i in range(len(PLACES))])


def shards(half_green, rotated_chol, chol_vectors, walkers, field_levels):
    f32, bf16 = jnp.float32, jnp.bfloat16
    own, own_rows, basis = chol_vectors.shape
    number = field_levels.shape[0]
    occupied, width = walkers.shape[1], walkers.shape[2]
    share = number // MATES
    rows = own_rows // CHIPS
    index = lax.axis_index("chol")
    core = index % 2
    zl = index // (2 * SIDE) % 2

    def by_number(array):
        array = array.reshape((2, 2) + array.shape[1:])
        array = jnp.where(core == 0, array, jnp.stack([array[:, 1], array[:, 0]], axis=1))
        return jnp.where(zl == 0, array, jnp.stack([array[1], array[0]], axis=0))

    green = jnp.broadcast_to(half_green, (len(GREEN[0]), occupied, width))
    green = lax.all_to_all(green, "chol", 0, 0, axis_index_groups=GREEN)

    levels = jnp.pad(field_levels.astype(bf16).T, ((0, occupied - own), (0, 0)))
    sent = jnp.concatenate([rotated_chol, levels[None]], axis=0)
    held = [sent, to_mate(sent, 1), to_mate(sent, 2)]

    chol_rows = chol_vectors.reshape(own * 2, CHIPS, rows // 2 * basis).transpose(1, 0, 2)
    chol_rows = with_layout_constraint(chol_rows, Layout((0, 1, 2)))

    green, chol_rows, held = lax.optimization_barrier((green, chol_rows, held))
    chol_mine = lax.all_to_all(chol_rows, "chol", 0, 0, axis_index_groups=PLANE)
    chol_mine = chol_mine.reshape(CHIPS * own * 2, rows // 2 * basis)

    held.append(to_mate(held[2], 1))
    levels = jnp.concatenate([h[own, : own + 1] for h in held], axis=0)
    chosen = lax.dynamic_index_in_dim(jnp.asarray(SHARES, bf16), zl * 2 + core, 0, keepdims=False)
    levels = jnp.dot(levels, chosen, preferred_element_type=f32)

    rotated = jnp.concatenate(held, axis=0)
    partial_bias = jnp.einsum("giq,wiq->gw", rotated, green, preferred_element_type=f32)
    partial_bias = jnp.pad(partial_bias.astype(bf16), ((0, 0), (0, width - share)))
    gathered = lax.all_gather(
        jnp.concatenate([walkers[0], partial_bias], axis=0), "orb", axis=0, tiled=False
    )
    bias = jnp.sum(gathered[:, occupied:, :share].astype(f32), axis=0)
    walker_full = gathered[:, :occupied]
    bias, chol_mine, walker_full = lax.optimization_barrier((bias, chol_mine, walker_full))

    aux_field = (LEVEL_SCALE * levels - TAU_ROOT * bias).astype(bf16)
    aux_field = aux_field.reshape(2, 2, own + 1, share)[:, :, :own]
    aux_field = jnp.where(zl == 0, aux_field, jnp.stack([aux_field[1], aux_field[0]]))
    zero = jnp.zeros_like(aux_field)
    aux_field = jnp.stack(
        [jnp.concatenate([aux_field, zero], axis=3), jnp.concatenate([zero, aux_field], axis=3)],
        axis=3,
    ).reshape(2, 2 * own * 2, 2 * share)
    aux_sent = jnp.broadcast_to(aux_field[None, :, None], (SIDE, 2, SIDE) + aux_field.shape[1:])
    aux_sent = aux_sent.reshape((CHIPS * 2,) + aux_field.shape[1:])
    aux_all = lax.all_to_all(aux_sent, "chol", 0, 0, axis_index_groups=BLOCK)
    aux_all = aux_all.reshape(SIDE, 2, SIDE, 2, own * 2, 2 * share)
    aux_all = jnp.concatenate([aux_all[:, 0], aux_all[:, 1]], axis=4)
    aux_all = aux_all.reshape(CHIPS, 2, own * 2, 4 * share)
    chol_others = to_mate(chol_mine, 1)
    potential = sum(
        lax.dot_general(
            aux_all[:, i].reshape(CHIPS * own * 2, 4 * share),
            part,
            (((0,), (0,)), ((), ())),
            preferred_element_type=f32,
        )
        for i, part in enumerate((chol_mine, chol_others))
    )
    potential = potential.astype(bf16).reshape(2, 2, SIDE * 2, SIDE, rows // 2 * basis)
    potential = potential.transpose(2, 0, 3, 1, 4).reshape(HOMES, rows, basis)
    parts = lax.all_to_all(potential, "chol", 0, 0, axis_index_groups=HOME)
    parts = parts.reshape(SIDE, SIDE, SIDE, rows, basis)
    total = jnp.sum(parts.astype(f32), axis=1).astype(bf16)
    total = total.reshape(CHIPS, 2, rows // 2, basis).transpose(1, 0, 2, 3)

    applied = jnp.einsum(
        "biq,pbq->ip",
        walker_full,
        total.reshape(own_rows, basis // width, width),
        preferred_element_type=f32,
    )
    new_walkers = (walkers[0].astype(f32) - TAU_ROOT * applied).astype(bf16)[None]

    bias = bias.reshape(MATES, own + 1, share)[:, :own]
    bias = [bias[0]] + [to_mate(bias[r], r) for r in range(1, MATES)]
    bias = by_number(jnp.stack(bias)).reshape(2, 2, own, SIDE, 2, SIDE)
    force_bias = bias.transpose(3, 4, 0, 5, 1, 2).reshape(number, own)
    return (force_bias, new_walkers)


def solution(mesh):
    placed = (
        P("chol", None, "orb"),
        P("chol", None, "orb"),
        P("chol", "orb", None),
        P("chol", None, "orb"),
        P(None, "chol"),
    )
    return jax.shard_map(
        shards,
        mesh=mesh,
        in_specs=placed,
        out_specs=(P(None, "chol"), P("chol", None, "orb")),
        check_vma=False,
    )
```

```python
import jax
import jax.numpy as jnp
import numpy as np
from jax import lax
from jax.experimental.layout import Layout, with_layout_constraint
from jax.sharding import PartitionSpec as P

LEVEL_SCALE = 1.7320508
TAU_ROOT = 0.2236068

SIDE = 4
MATES = 4
PLACES = [
    (y, zh, zl, x, core)
    for y in range(SIDE)
    for zh in range(2)
    for zl in range(2)
    for x in range(SIDE)
    for core in range(2)
]


def groups_of(fixed, order):
    found = {}
    for index, place in enumerate(PLACES):
        key = tuple(place[i] for i in fixed)
        found.setdefault(key, []).append((tuple(place[i] for i in order), index))
    return [[index for _, index in sorted(members)] for members in found.values()]


Y, ZH, ZL, X, CORE = range(5)
GREEN = groups_of((ZL, CORE), (Y, ZH, X))
PLANE = groups_of((ZH, ZL, CORE), (Y, X))
LINE = groups_of((Y, ZH, ZL, CORE), (X,))
BLOCK = groups_of((ZH, X, CORE), (Y, ZL))
HOME = groups_of((CORE,), (Y, ZH, ZL, X))
HOMES = len(HOME[0])
CHIPS = len(PLANE[0])
SHARES = np.zeros((MATES, len(PLACES), len(GREEN[0])), np.float32)
for group in GREEN:
    first = PLACES[group[0]]
    SHARES[first[ZL] * 2 + first[CORE], group, np.arange(len(group))] = 1


def to_mate(array, number):
    step = (number & 1) + (number >> 1) * 2 * SIDE
    return lax.ppermute(array, "chol", [(i, i ^ step) for i in range(len(PLACES))])


def shards(half_green, rotated_chol, chol_vectors, walkers, field_levels):
    f32, bf16 = jnp.float32, jnp.bfloat16
    own, own_rows, basis = chol_vectors.shape
    number = field_levels.shape[0]
    occupied, width = walkers.shape[1], walkers.shape[2]
    share = number // MATES
    rows = own_rows // CHIPS
    index = lax.axis_index("chol")
    core = index % 2
    zl = index // (2 * SIDE) % 2

    def by_number(array):
        array = array.reshape((2, 2) + array.shape[1:])
        array = jnp.where(core == 0, array, jnp.stack([array[:, 1], array[:, 0]], axis=1))
        return jnp.where(zl == 0, array, jnp.stack([array[1], array[0]], axis=0))

    green = jnp.broadcast_to(half_green, (len(GREEN[0]), occupied, width))
    green = lax.all_to_all(green, "chol", 0, 0, axis_index_groups=GREEN)

    levels = jnp.pad(field_levels.astype(bf16).T, ((0, occupied - own), (0, 0)))
    sent = jnp.concatenate([rotated_chol, levels[None]], axis=0)
    held = [sent, to_mate(sent, 1), to_mate(sent, 2)]

    chol_rows = chol_vectors.reshape(own * 2, CHIPS, rows // 2 * basis).transpose(1, 0, 2)
    chol_rows = with_layout_constraint(chol_rows, Layout((0, 1, 2)))

    green, chol_rows, held = lax.optimization_barrier((green, chol_rows, held))
    chol_mine = lax.all_to_all(chol_rows, "chol", 0, 0, axis_index_groups=PLANE)
    chol_mine = chol_mine.reshape(CHIPS * own * 2, rows // 2 * basis)

    held.append(to_mate(held[2], 1))
    levels = jnp.concatenate([h[own, : own + 1] for h in held], axis=0)
    chosen = lax.dynamic_index_in_dim(jnp.asarray(SHARES, bf16), zl * 2 + core, 0, keepdims=False)
    levels = jnp.dot(levels, chosen, preferred_element_type=f32)

    rotated = jnp.concatenate(held, axis=0)
    partial_bias = jnp.einsum("giq,wiq->gw", rotated, green, preferred_element_type=f32)
    upper = lax.reduce_precision(partial_bias, 8, 7)
    partial_bias = jnp.concatenate([upper, partial_bias - upper], axis=1).astype(bf16)
    partial_bias = jnp.pad(partial_bias, ((0, 0), (0, width - 2 * share)))
    partial_bias, levels = lax.optimization_barrier((partial_bias, levels))
    gathered = lax.all_gather(
        jnp.concatenate([walkers[0], partial_bias], axis=0), "orb", axis=0, tiled=False
    )
    bias = jnp.sum(gathered[:, occupied:, : 2 * share].astype(f32), axis=0)
    bias = bias[:, :share] + bias[:, share:]
    walker_full = gathered[:, :occupied]
    aux_field = (LEVEL_SCALE * levels - TAU_ROOT * bias).astype(bf16)
    aux_field = aux_field.reshape(2, 2, own + 1, share)[:, :, :own]
    aux_field = jnp.where(zl == 0, aux_field, jnp.stack([aux_field[1], aux_field[0]]))
    zero = jnp.zeros_like(aux_field)
    aux_field = jnp.stack(
        [jnp.concatenate([aux_field, zero], axis=3), jnp.concatenate([zero, aux_field], axis=3)],
        axis=3,
    ).reshape(2, 2 * own * 2, 2 * share)
    aux_field = lax.all_gather(aux_field, "chol", axis=1, axis_index_groups=LINE, tiled=False)
    aux_field, chol_mine, bias = lax.optimization_barrier((aux_field, chol_mine, bias))
    aux_sent = jnp.broadcast_to(aux_field[None], (SIDE,) + aux_field.shape)
    aux_sent = aux_sent.reshape(SIDE * 2, SIDE * 2 * own * 2, 2 * share)
    aux_all = lax.all_to_all(aux_sent, "chol", 0, 0, axis_index_groups=BLOCK)
    aux_all = aux_all.reshape(SIDE, 2, SIDE, 2, own * 2, 2 * share)
    aux_all = jnp.concatenate([aux_all[:, 0], aux_all[:, 1]], axis=4)
    aux_all = aux_all.reshape(CHIPS, 2, own * 2, 4 * share)
    chol_others = to_mate(chol_mine, 1)
    potential = sum(
        lax.dot_general(
            aux_all[:, i].reshape(CHIPS * own * 2, 4 * share),
            part,
            (((0,), (0,)), ((), ())),
            preferred_element_type=f32,
        )
        for i, part in enumerate((chol_mine, chol_others))
    )
    potential = potential.astype(bf16).reshape(2, 2, SIDE * 2, SIDE, rows // 2 * basis)
    potential = potential.transpose(2, 0, 3, 1, 4).reshape(HOMES, rows, basis)
    parts = lax.all_to_all(potential, "chol", 0, 0, axis_index_groups=HOME)
    parts = parts.reshape(SIDE, SIDE, SIDE, rows, basis)
    total = jnp.sum(parts.astype(f32), axis=1).astype(bf16)
    total = total.reshape(CHIPS, 2, rows // 2, basis).transpose(1, 0, 2, 3)

    applied = jnp.einsum(
        "biq,pbq->ip",
        walker_full,
        total.reshape(own_rows, basis // width, width),
        preferred_element_type=f32,
    )
    new_walkers = (walkers[0].astype(f32) - TAU_ROOT * applied).astype(bf16)[None]

    bias = bias.reshape(MATES, own + 1, share)[:, :own]
    bias = [bias[0]] + [to_mate(bias[r], r) for r in range(1, MATES)]
    bias = by_number(jnp.stack(bias)).reshape(2, 2, own, SIDE, 2, SIDE)
    force_bias = bias.transpose(3, 4, 0, 5, 1, 2).reshape(number, own)
    return (force_bias, new_walkers)


def solution(mesh):
    placed = (
        P("chol", None, "orb"),
        P("chol", None, "orb"),
        P("chol", "orb", None),
        P("chol", None, "orb"),
        P(None, "chol"),
    )
    return jax.shard_map(
        shards,
        mesh=mesh,
        in_specs=placed,
        out_specs=(P(None, "chol"), P("chol", None, "orb")),
        check_vma=False,
    )
```

```python
import jax
import jax.numpy as jnp
import numpy as np
from jax import lax
from jax.experimental.layout import Layout, with_layout_constraint
from jax.sharding import PartitionSpec as P

LEVEL_SCALE = 1.7320508
TAU_ROOT = 0.2236068

SIDE = 4
MATES = 4
PLACES = [
    (y, zh, zl, x, core)
    for y in range(SIDE)
    for zh in range(2)
    for zl in range(2)
    for x in range(SIDE)
    for core in range(2)
]


def groups_of(fixed, order):
    found = {}
    for index, place in enumerate(PLACES):
        key = tuple(place[i] for i in fixed)
        found.setdefault(key, []).append((tuple(place[i] for i in order), index))
    return [[index for _, index in sorted(members)] for members in found.values()]


Y, ZH, ZL, X, CORE = range(5)
GREEN = groups_of((ZL, CORE), (Y, ZH, X))
PLANE = groups_of((ZH, ZL, CORE), (Y, X))
BLOCK = groups_of((ZH, CORE), (Y, ZL, X))
HOME = groups_of((CORE,), (Y, ZH, ZL, X))
HOMES = len(HOME[0])
CHIPS = len(PLANE[0])
SHARES = np.zeros((MATES, len(PLACES), len(GREEN[0])), np.float32)
for group in GREEN:
    first = PLACES[group[0]]
    SHARES[first[ZL] * 2 + first[CORE], group, np.arange(len(group))] = 1


def to_mate(array, number):
    step = (number & 1) + (number >> 1) * 2 * SIDE
    return lax.ppermute(array, "chol", [(i, i ^ step) for i in range(len(PLACES))])


def shards(half_green, rotated_chol, chol_vectors, walkers, field_levels):
    f32, bf16 = jnp.float32, jnp.bfloat16
    own, own_rows, basis = chol_vectors.shape
    number = field_levels.shape[0]
    occupied, width = walkers.shape[1], walkers.shape[2]
    share = number // MATES
    rows = own_rows // CHIPS
    index = lax.axis_index("chol")
    core = index % 2
    zl = index // (2 * SIDE) % 2

    def by_number(array):
        array = array.reshape((2, 2) + array.shape[1:])
        array = jnp.where(core == 0, array, jnp.stack([array[:, 1], array[:, 0]], axis=1))
        return jnp.where(zl == 0, array, jnp.stack([array[1], array[0]], axis=0))

    green = jnp.broadcast_to(half_green, (len(GREEN[0]), occupied, width))
    green = lax.all_to_all(green, "chol", 0, 0, axis_index_groups=GREEN)

    levels = jnp.pad(field_levels.astype(bf16).T, ((0, occupied - own), (0, 0)))
    sent = jnp.concatenate([rotated_chol, levels[None]], axis=0)
    held = [sent, to_mate(sent, 1), to_mate(sent, 2)]

    chol_rows = chol_vectors.reshape(own * 2, CHIPS, rows // 2 * basis).transpose(1, 0, 2)
    chol_rows = with_layout_constraint(chol_rows, Layout((0, 1, 2)))

    green, chol_rows, held[1] = lax.optimization_barrier((green, chol_rows, held[1]))
    chol_mine = lax.all_to_all(chol_rows, "chol", 0, 0, axis_index_groups=PLANE)
    chol_mine = chol_mine.reshape(CHIPS * own * 2, rows // 2 * basis)

    held.append(to_mate(held[2], 1))
    levels = jnp.concatenate([h[own, : own + 1] for h in held], axis=0)
    chosen = lax.dynamic_index_in_dim(jnp.asarray(SHARES, bf16), zl * 2 + core, 0, keepdims=False)
    levels = jnp.dot(levels, chosen, preferred_element_type=f32)

    rotated = jnp.concatenate(held, axis=0)
    partial_bias = jnp.einsum("giq,wiq->gw", rotated, green, preferred_element_type=f32)
    upper = lax.reduce_precision(partial_bias, 8, 7)
    partial_bias = jnp.concatenate([upper, partial_bias - upper], axis=1).astype(bf16)
    partial_bias = jnp.pad(partial_bias, ((0, 0), (0, width - 2 * share)))
    gathered = lax.all_gather(
        jnp.concatenate([walkers[0], partial_bias], axis=0), "orb", axis=0, tiled=False
    )
    bias = jnp.sum(gathered[:, occupied:, : 2 * share].astype(f32), axis=0)
    bias = bias[:, :share] + bias[:, share:]
    walker_full = gathered[:, :occupied]
    bias, levels, chol_mine, walker_full = lax.optimization_barrier(
        (bias, levels, chol_mine, walker_full)
    )

    aux_field = (LEVEL_SCALE * levels - TAU_ROOT * bias).astype(bf16)
    aux_field = aux_field.reshape(2, 2, own + 1, share)[:, :, :own]
    aux_field = jnp.where(zl == 0, aux_field, jnp.stack([aux_field[1], aux_field[0]]))
    zero = jnp.zeros_like(aux_field)
    aux_field = jnp.stack(
        [jnp.concatenate([aux_field, zero], axis=3), jnp.concatenate([zero, aux_field], axis=3)],
        axis=3,
    ).reshape(2, 2 * own * 2, 2 * share)
    aux_sent = jnp.broadcast_to(aux_field[None, :, None], (SIDE, 2, SIDE) + aux_field.shape[1:])
    aux_sent = aux_sent.reshape((CHIPS * 2,) + aux_field.shape[1:])
    aux_all = lax.all_to_all(aux_sent, "chol", 0, 0, axis_index_groups=BLOCK)
    aux_all = aux_all.reshape(SIDE, 2, SIDE, 2, own * 2, 2 * share)
    aux_all = jnp.concatenate([aux_all[:, 0], aux_all[:, 1]], axis=4)
    aux_all = aux_all.reshape(CHIPS, 2, own * 2, 4 * share)
    chol_others = to_mate(chol_mine, 1)
    potential = sum(
        lax.dot_general(
            aux_all[:, i].reshape(CHIPS * own * 2, 4 * share),
            part,
            (((0,), (0,)), ((), ())),
            preferred_element_type=f32,
        )
        for i, part in enumerate((chol_mine, chol_others))
    )
    potential = potential.astype(bf16).reshape(2, 2, SIDE * 2, SIDE, rows // 2 * basis)
    potential = potential.transpose(2, 0, 3, 1, 4).reshape(HOMES, 2, rows // 2 * basis)
    parts = lax.all_to_all(potential, "chol", 0, 0, axis_index_groups=HOME)
    parts = parts.reshape(SIDE, SIDE, SIDE, 2, rows // 2 * basis)
    total = jnp.sum(parts.astype(f32), axis=1).astype(bf16)
    total = total.reshape(CHIPS, 2, rows // 2, basis).transpose(1, 0, 2, 3)

    applied = jnp.einsum(
        "biq,pbq->ip",
        walker_full,
        total.reshape(own_rows, basis // width, width),
        preferred_element_type=f32,
    )
    new_walkers = (walkers[0].astype(f32) - TAU_ROOT * applied).astype(bf16)[None]

    bias = bias.reshape(MATES, own + 1, share)[:, :own]
    bias = [bias[0]] + [to_mate(bias[r], r) for r in range(1, MATES)]
    bias = by_number(jnp.stack(bias)).reshape(2, 2, own, SIDE, 2, SIDE)
    force_bias = bias.transpose(3, 4, 0, 5, 1, 2).reshape(number, own)
    return (force_bias, new_walkers)


def solution(mesh):
    placed = (
        P("chol", None, "orb"),
        P("chol", None, "orb"),
        P("chol", "orb", None),
        P("chol", None, "orb"),
        P(None, "chol"),
    )
    return jax.shard_map(
        shards,
        mesh=mesh,
        in_specs=placed,
        out_specs=(P(None, "chol"), P("chol", None, "orb")),
        check_vma=False,
    )
```

```python
import jax
import jax.numpy as jnp
import numpy as np
from jax import lax
from jax.experimental.layout import Layout, with_layout_constraint
from jax.sharding import PartitionSpec as P

LEVEL_SCALE = 1.7320508
TAU_ROOT = 0.2236068

SIDE = 4
MATES = 4
PLACES = [
    (y, zh, zl, x, core)
    for y in range(SIDE)
    for zh in range(2)
    for zl in range(2)
    for x in range(SIDE)
    for core in range(2)
]


def groups_of(fixed, order):
    found = {}
    for index, place in enumerate(PLACES):
        key = tuple(place[i] for i in fixed)
        found.setdefault(key, []).append((tuple(place[i] for i in order), index))
    return [[index for _, index in sorted(members)] for members in found.values()]


Y, ZH, ZL, X, CORE = range(5)
GREEN = groups_of((ZL, CORE), (Y, ZH, X))
PLANE = groups_of((ZH, ZL, CORE), (Y, X))
BLOCK = groups_of((ZH, CORE), (Y, ZL, X))
HOME = groups_of((CORE,), (Y, ZH, ZL, X))
HOMES = len(HOME[0])
CHIPS = len(PLANE[0])
SHARES = np.zeros((MATES, len(PLACES), len(GREEN[0])), np.float32)
for group in GREEN:
    first = PLACES[group[0]]
    SHARES[first[ZL] * 2 + first[CORE], group, np.arange(len(group))] = 1


def to_mate(array, number):
    step = (number & 1) + (number >> 1) * 2 * SIDE
    return lax.ppermute(array, "chol", [(i, i ^ step) for i in range(len(PLACES))])


def shards(half_green, rotated_chol, chol_vectors, walkers, field_levels):
    f32, bf16 = jnp.float32, jnp.bfloat16
    own, own_rows, basis = chol_vectors.shape
    number = field_levels.shape[0]
    occupied, width = walkers.shape[1], walkers.shape[2]
    share = number // MATES
    rows = own_rows // CHIPS
    index = lax.axis_index("chol")
    core = index % 2
    zl = index // (2 * SIDE) % 2

    def by_number(array):
        array = array.reshape((2, 2) + array.shape[1:])
        array = jnp.where(core == 0, array, jnp.stack([array[:, 1], array[:, 0]], axis=1))
        return jnp.where(zl == 0, array, jnp.stack([array[1], array[0]], axis=0))

    green = jnp.broadcast_to(half_green, (len(GREEN[0]), occupied, width))
    green = lax.all_to_all(green, "chol", 0, 0, axis_index_groups=GREEN)

    levels = jnp.pad(field_levels.astype(bf16).T, ((0, occupied - own), (0, 0)))
    sent = jnp.concatenate([rotated_chol, levels[None]], axis=0)
    held = [sent, to_mate(sent, 1)]

    chol_rows = chol_vectors.reshape(own * 2, CHIPS, rows // 2 * basis).transpose(1, 0, 2)
    chol_rows = with_layout_constraint(chol_rows, Layout((0, 1, 2)))

    green, chol_rows, held[0], held[1] = lax.optimization_barrier(
        (green, chol_rows, held[0], held[1])
    )
    chol_mine = lax.all_to_all(chol_rows, "chol", 0, 0, axis_index_groups=PLANE)
    chol_mine = chol_mine.reshape(CHIPS * own * 2, rows // 2 * basis)

    held.append(to_mate(held[0], 2))
    held.append(to_mate(held[2], 1))
    levels = jnp.concatenate([h[own, : own + 1] for h in held], axis=0)
    chosen = lax.dynamic_index_in_dim(jnp.asarray(SHARES, bf16), zl * 2 + core, 0, keepdims=False)
    levels = jnp.dot(levels, chosen, preferred_element_type=f32)

    rotated = jnp.concatenate(held, axis=0)
    partial_bias = jnp.einsum("giq,wiq->gw", rotated, green, preferred_element_type=f32)
    upper = lax.reduce_precision(partial_bias, 8, 7)
    partial_bias = jnp.concatenate([upper, partial_bias - upper], axis=1).astype(bf16)
    partial_bias = jnp.pad(partial_bias, ((0, 0), (0, width - 2 * share)))
    gathered = lax.all_gather(
        jnp.concatenate([walkers[0], partial_bias], axis=0), "orb", axis=0, tiled=False
    )
    bias = jnp.sum(gathered[:, occupied:, : 2 * share].astype(f32), axis=0)
    bias = bias[:, :share] + bias[:, share:]
    walker_full = gathered[:, :occupied]
    bias, levels, chol_mine, walker_full = lax.optimization_barrier(
        (bias, levels, chol_mine, walker_full)
    )

    aux_field = (LEVEL_SCALE * levels - TAU_ROOT * bias).astype(bf16)
    aux_field = aux_field.reshape(2, 2, own + 1, share)[:, :, :own]
    aux_field = jnp.where(zl == 0, aux_field, jnp.stack([aux_field[1], aux_field[0]]))
    zero = jnp.zeros_like(aux_field)
    aux_field = jnp.stack(
        [jnp.concatenate([aux_field, zero], axis=3), jnp.concatenate([zero, aux_field], axis=3)],
        axis=3,
    ).reshape(2, 2 * own * 2, 2 * share)
    aux_sent = jnp.broadcast_to(aux_field[None, :, None], (SIDE, 2, SIDE) + aux_field.shape[1:])
    aux_sent = aux_sent.reshape((CHIPS * 2,) + aux_field.shape[1:])
    aux_all = lax.all_to_all(aux_sent, "chol", 0, 0, axis_index_groups=BLOCK)
    aux_all = aux_all.reshape(SIDE, 2, SIDE, 2, own * 2, 2 * share)
    aux_all = jnp.concatenate([aux_all[:, 0], aux_all[:, 1]], axis=4)
    aux_all = aux_all.reshape(CHIPS, 2, own * 2, 4 * share)
    chol_others = to_mate(chol_mine, 1)
    potential = sum(
        lax.dot_general(
            aux_all[:, i].reshape(CHIPS * own * 2, 4 * share),
            part,
            (((0,), (0,)), ((), ())),
            preferred_element_type=f32,
        )
        for i, part in enumerate((chol_mine, chol_others))
    )
    potential = potential.astype(bf16).reshape(2, 2, SIDE * 2, SIDE, rows // 2 * basis)
    potential = potential.transpose(2, 0, 3, 1, 4).reshape(HOMES, 2, rows // 2 * basis)
    parts = lax.all_to_all(potential, "chol", 0, 0, axis_index_groups=HOME)
    parts = parts.reshape(SIDE, SIDE, SIDE, 2, rows // 2 * basis)
    total = jnp.sum(parts.astype(f32), axis=1).astype(bf16)
    total = total.reshape(CHIPS, 2, rows // 2, basis).transpose(1, 0, 2, 3)

    applied = jnp.einsum(
        "biq,pbq->ip",
        walker_full,
        total.reshape(own_rows, basis // width, width),
        preferred_element_type=f32,
    )
    new_walkers = (walkers[0].astype(f32) - TAU_ROOT * applied).astype(bf16)[None]

    bias = bias.reshape(MATES, own + 1, share)[:, :own]
    bias = [bias[0]] + [to_mate(bias[r], r) for r in range(1, MATES)]
    bias = by_number(jnp.stack(bias)).reshape(2, 2, own, SIDE, 2, SIDE)
    force_bias = bias.transpose(3, 4, 0, 5, 1, 2).reshape(number, own)
    return (force_bias, new_walkers)


def solution(mesh):
    placed = (
        P("chol", None, "orb"),
        P("chol", None, "orb"),
        P("chol", "orb", None),
        P("chol", None, "orb"),
        P(None, "chol"),
    )
    return jax.shard_map(
        shards,
        mesh=mesh,
        in_specs=placed,
        out_specs=(P(None, "chol"), P("chol", None, "orb")),
        check_vma=False,
    )
```
